32 devices in a mesh: expert: 16 (over z, y, core), hidden: 2 (over x).
Axes of the slice: x: 2, y: 2, z: 4, core: 2. Of those that a mesh axis runs over, the one named last changes fastest.
Arguments:
- tokens: bfloat16 [256, 3584], P(('expert', 'hidden')), may hold values from -6 to 6
- routes: int32 [256, 8], P(('expert', 'hidden')), may hold values from 0 to 15, all different within a row; in each aligned block of 16 rows (0 to 15, 16 to 31, ...) at most 16 rows name the same one
- gate_weights: bfloat16 [256, 8], P(('expert', 'hidden')), may hold values from 0.049804688 to 0.59765625
- w_in: bfloat16 [16, 3584, 1024], P('expert', None, 'hidden'), may hold values from -0.09375 to 0.09375
- w_out: bfloat16 [16, 1024, 3584], P('expert', 'hidden'), may hold values from -0.1875 to 0.1875
Outputs:
- mixed: bfloat16 [256, 3584], P(('expert', 'hidden'))
The draws below stay inside these ranges and needn't reach their ends.
Inputs may be any that keep to these rules, and one draw needn't show every extreme that they name: `routes`: the 8 experts of a token differ. In each aligned block of 16 tokens no expert is named by more than 16 tokens, a bound that some block reaches.
All inputs are finite; a program needn't handle non-finite values.
Results may differ from the reference program's by a relative error of at most 0.01.
Values may be sent and summed in bfloat16 or wider, within the bound.
A program may use at most 64 MiB of HBM per device.

```python
import math
import jax
import jax.numpy as jnp
import numpy as np
from jax import lax

D = 3584
FF = 1024
TOP = 8
EXPERTS = 16
GROUP = 16
TOKENS = 256
CAP = 16
FF_PART = 512
N_HIDDEN = 2


def block_levels(rng, extent, split, smallest, high):
    loudness = 1.0
    for dim, shards_of in split:
        steps = jax.random.uniform(jax.random.fold_in(jax.random.fold_in(rng, 6), dim), (shards_of,), jnp.float32, smallest / len(split), high / len(split))
        loudness = loudness * jnp.repeat(jnp.exp(steps), extent[dim] // shards_of).reshape((-1,) + (1,) * (len(extent) - 1 - dim))
    return loudness


def deal_out(stream_key, own, number, rows, count, top, reach, skew):
    order = jax.random.permutation(stream_key, count)
    packed, usual = load_shares(count, rows * top, reach, skew, True), load_shares(count, rows * top, reach, skew, False)
    places = jnp.arange(count)

    def named(tallies, turn):
        used = int((tallies > 0).sum())
        fixed = max(1, used // 4)
        shifted = fixed + (places - fixed + turn * (used - fixed)) % max(1, count - fixed)
        return jnp.zeros((count,), jnp.int32).at[order[jnp.where(places < fixed, places, shifted)]].set(jnp.asarray(tallies, jnp.int32))

    tallies = jnp.where(number % 4 == 0, named(packed, number // 4), named(usual, number - number // 4 - 1))
    mixed = jax.random.permutation(jax.random.fold_in(own, 3), count)
    source_of, taker = mixed[0:count // 2 * 2:2], mixed[1:count // 2 * 2:2]
    slack = jnp.minimum(tallies[source_of] - 1, reach - tallies[taker]) // 2
    slack = jnp.where((source_of == order[0]) | (taker == order[0]) | (tallies[taker] == 0), 0, jnp.maximum(slack, 0))
    shifted = jax.random.randint(jax.random.fold_in(own, 4), (count // 2,), 0, 1 << 20) % (slack + 1)
    tallies = tallies.at[source_of].add(-shifted).at[taker].add(shifted)
    labels = jnp.searchsorted(jnp.cumsum(tallies), jnp.arange(rows * top), side="right").astype(jnp.int32)
    grid = labels.reshape(top, rows).T
    grid = grid[jax.random.permutation(jax.random.fold_in(own, 1), rows)]
    turn = jax.random.randint(jax.random.fold_in(own, 2), (rows, 1), 0, top)
    return jnp.take_along_axis(grid, (jnp.arange(top)[None, :] + turn) % top, axis=1)


def load_shares(number_of, total, reach, skew, full):
    portions = [(1 << 20) // math.isqrt(grade ** skew) + 1 for grade in range(1, number_of + 1)]
    largest = reach if full else min(reach, max(-(-total // number_of), total * portions[0] // sum(portions)))
    least = 1 if total - largest >= number_of - 1 else 0
    given, spare = [largest] + [least] * (number_of - 1), total - largest - least * (number_of - 1)
    while spare > 0:
        candidates = [i for i in range(1, number_of) if given[i] < largest] or [i for i in range(1, number_of) if given[i] < reach]
        pool, remaining = sum([portions[i] for i in candidates]), spare
        for i in candidates:
            more = min(reach - given[i], max(1, remaining * portions[i] // pool), spare)
            given[i] = given[i] + more
            spare = spare - more
    return np.array(given)


def gaussian(own_key, shape, width, reach, split=(), kind=jnp.bfloat16):
    drawn = jax.random.normal(own_key, shape, jnp.float32) * width
    if len(split) > 0:
        drawn = block_levels(own_key, shape, split, -0.22, 0.18) * drawn
    return jnp.clip(drawn, min=-reach, max=reach).astype(kind)


def setup_inputs(seed: int = 0) -> dict:
    keys = jax.random.split(jax.random.key(seed), 6)
    tokens = gaussian(keys[0], (TOKENS, D), 1.0, 6.0, ((0, 32),))
    routes_keys = jax.random.split(jax.random.fold_in(keys[1], 1), TOKENS // GROUP)
    routes_turns = jax.random.permutation(jax.random.fold_in(keys[1], 3), TOKENS // GROUP)
    routes = jax.vmap(lambda own, number: deal_out(jax.random.fold_in(keys[1], 2), own, number, GROUP, EXPERTS, TOP, CAP, 2))(routes_keys, routes_turns).reshape((TOKENS, TOP))
    gate_weights = jnp.clip(jnp.exp(math.log(0.59765625) - 2.4849066 * jax.random.uniform(keys[2], (TOKENS, TOP), jnp.float32) ** block_levels(keys[2], (TOKENS, TOP), ((0, 32),), -0.2, 0.2)), 0.049804688, 0.59765625).astype(jnp.bfloat16)
    w_in = gaussian(keys[3], (EXPERTS, D, FF), D ** -0.5, 0.09375, ((0, 16), (2, 2)))
    w_out = gaussian(keys[4], (EXPERTS, FF, D), FF ** -0.5, 0.1875, ((0, 16), (1, 2)))
    return {"tokens": tokens, "routes": routes, "gate_weights": gate_weights, "w_in": w_in, "w_out": w_out}


def reference(tokens, routes, gate_weights, w_in, w_out):
    groups = TOKENS // GROUP
    items = GROUP * TOP
    slots = EXPERTS * CAP
    expert_ids = routes.reshape(groups, items).astype(jnp.int32)
    onehot = (expert_ids[:, :, None] == jnp.arange(EXPERTS).astype(jnp.int32)[None, None, :]).astype(jnp.int32)
    before = jnp.cumsum(onehot, axis=1) - onehot
    rank = jnp.sum(before * onehot, axis=2).astype(jnp.int32)
    slot = expert_ids * CAP + rank
    local_row = (jnp.arange(items).astype(jnp.int32) // TOP).astype(jnp.int32)
    gates = gate_weights.reshape(groups, items).astype(jnp.float32)
    match = slot[:, None, :] == jnp.arange(slots).astype(jnp.int32)[None, :, None]
    source_row = jnp.sum(jnp.where(match, local_row[None, None, :], 0), axis=2).astype(jnp.int32)
    source_row = source_row + (jnp.arange(groups).astype(jnp.int32) * GROUP)[:, None]
    slot_gate = jnp.sum(jnp.where(match, gates[:, None, :], jnp.float32(0.0)), axis=2)
    source_row = source_row.reshape(groups, EXPERTS, CAP).transpose(1, 0, 2).reshape(EXPERTS, groups * CAP)
    slot_gate = slot_gate.reshape(groups, EXPERTS, CAP).transpose(1, 0, 2).reshape(EXPERTS, groups * CAP)

    def one_expert(total, inputs):
        w_first, w_second, rows, weights = inputs
        picked = tokens[rows]
        hidden = jax.nn.silu(jnp.dot(picked, w_first, preferred_element_type=jnp.float32)).astype(jnp.bfloat16)
        blocks = hidden.reshape(hidden.shape[0], N_HIDDEN, FF_PART).astype(jnp.float32)
        second = w_second.reshape(N_HIDDEN, FF_PART, D).astype(jnp.float32)
        partial_value = jnp.einsum("rhf,hfd->hrd", blocks, second).astype(jnp.bfloat16)
        out_rows = jnp.sum(partial_value.astype(jnp.float32), axis=0)
        total = total.at[rows].add(weights[:, None] * out_rows)
        return total, None

    start = jnp.zeros((TOKENS, D), jnp.float32)
    total, _ = lax.scan(one_expert, start, (w_in, w_out, source_row, slot_gate))
    return total.astype(jnp.bfloat16)
```

```python
import functools

import jax
import jax.numpy as jnp
from jax import lax
from jax.experimental import pallas as pl
from jax.experimental.pallas import tpu as pltpu
from jax.sharding import PartitionSpec as P

MESH = pl.DeviceIdType.MESH
F32 = jnp.float32
BF16 = jnp.bfloat16


def routed_plan(tokens, routes, gate_weights, w_in, w_out):
    group_x, group_routes, group_gates = (
        lax.all_gather(tokens, "hidden", axis=0, tiled=True),
        lax.all_gather(routes, "hidden", axis=0, tiled=True),
        lax.all_gather(gate_weights, "hidden", axis=0, tiled=True),
    )
    group = group_x.shape[0]
    top = group_routes.shape[1]
    experts = w_in.shape[0] * lax.axis_size("expert")
    capacity = min(group, 2 * group * top // experts)
    items = group * top
    expert_ids = group_routes.reshape(items)
    onehot = (expert_ids[:, None] == jnp.arange(experts, dtype=jnp.int32)[None, :]).astype(
        jnp.int32
    )
    before = jnp.cumsum(onehot, axis=0) - onehot
    rank = jnp.sum(before * onehot, axis=1)
    slot = expert_ids * capacity + rank
    token_of_item = jnp.arange(items, dtype=jnp.int32) // top
    match = slot[None, :] == jnp.arange(experts * capacity, dtype=jnp.int32)[:, None]
    source_row = jnp.sum(jnp.where(match, token_of_item[None, :], 0), axis=1)
    filled = jnp.any(match, axis=1)
    buffer = jnp.where(filled[:, None], group_x[source_row], jnp.zeros((), jnp.bfloat16))
    buffer = buffer.reshape(experts, capacity, group_x.shape[1])
    first = w_in[0]
    second = w_out[0]
    rows = lax.all_to_all(buffer, "expert", split_axis=0, concat_axis=0, tiled=True)
    count = rows.shape[0] * rows.shape[1]
    flat = rows.reshape(count, rows.shape[2])
    hidden = jax.nn.silu(jnp.dot(flat, first, preferred_element_type=jnp.float32)).astype(
        jnp.bfloat16
    )
    partial_value = jnp.dot(hidden, second, preferred_element_type=jnp.float32)
    partial_value = partial_value.reshape(rows.shape[0], rows.shape[1], partial_value.shape[1])
    gates_flat = group_gates.reshape(items).astype(jnp.float32)
    summed = lax.psum_scatter(
        partial_value.astype(jnp.bfloat16), "hidden", scatter_dimension=2, tiled=True
    ).astype(jnp.float32)
    back = lax.all_to_all(
        summed.astype(jnp.bfloat16), "expert", split_axis=0, concat_axis=0, tiled=True
    ).astype(summed.dtype)
    width = back.shape[2]
    picked = back.reshape(experts * capacity, width)[slot]
    mixed_part = jnp.sum((picked * gates_flat[:, None]).reshape(group, top, width), axis=1)
    result = lax.all_to_all(
        mixed_part.astype(jnp.bfloat16), "hidden", split_axis=0, concat_axis=1, tiled=True
    ).astype(mixed_part.dtype)
    return result.astype(jnp.bfloat16)


def dense_kernel(
    zs, tok_ref, routes_ref, gates_ref, win_hbm, wout_hbm, out_ref,
    buf_a, buf_b, win, wout, gate, act,
    cs_a, cs_b, cr_a, cr_b, acc_a, acc_b,
    s1_a, s1_b, r1_a, r1_b, k1_a, k1_b,
    s2_a, s2_b, r2_a, r2_b, k2_a, k2_b,
    s3_a, s3_b, r3_a, r3_b,
    w_sem, gz_send, gz_recv, g_send, g_recv, r_send, r_recv, rz_send, rz_recv,
):
    bufs = (buf_a, buf_b)
    cs, cr, acc = (cs_a, cs_b), (cr_a, cr_b), (acc_a, acc_b)
    s1, r1, k1 = (s1_a, s1_b), (r1_a, r1_b), (k1_a, k1_b)
    s2, r2, k2 = (s2_a, s2_b), (r2_a, r2_b), (k2_a, k2_b)
    s3, r3 = (s3_a, s3_b), (r3_a, r3_b)
    e = lax.axis_index("expert")
    x = lax.axis_index("hidden")
    c = lax.rem(e, 2)
    y = lax.rem(e // 2, 2)
    z = e // 4
    rows, width = tok_ref.shape
    half = width // 2
    top = routes_ref.shape[1]

    def device(zz, yy, cc, xx):
        return ((zz * 2 + yy) * 2 + cc, xx)

    x_peer = device(z, y, c, 1 - x)
    y_peer = device(z, 1 - y, c, x)
    c_peer = device(z, y, 1 - c, x)
    z_peers = [device(lax.rem(z + d, zs), y, c, x) for d in range(1, zs)]

    load_in = pltpu.make_async_copy(win_hbm.at[0], win, w_sem.at[0])
    load_out = pltpu.make_async_copy(wout_hbm.at[0], wout, w_sem.at[1])
    load_in.start()
    load_out.start()

    barrier = pltpu.get_barrier_semaphore()
    for peer in z_peers + [x_peer, y_peer, c_peer]:
        pl.semaphore_signal(barrier, inc=1, device_id=peer, device_id_type=MESH)

    lanes = lax.broadcasted_iota(jnp.int32, (rows, 128), 1)
    table = jnp.zeros((rows, 128), F32)
    routes = routes_ref[...]
    gates = gates_ref[...].astype(F32)
    for k in range(top):
        table = table + jnp.where(lanes == routes[:, k : k + 1], gates[:, k : k + 1], 0.0)
    buf_a[c, x, y, z] = tok_ref[:, :half]
    buf_b[c, x, y, z, :, :half] = tok_ref[:, half:]
    buf_b[c, x, y, z, :, half:] = table.astype(BF16)

    pl.semaphore_wait(barrier, zs + 2)

    def remote(src, dst, send, recv, peer):
        return pltpu.make_async_remote_copy(
            src_ref=src, dst_ref=dst, send_sem=send, recv_sem=recv,
            device_id=peer, device_id_type=MESH,
        )

    started = []

    def go(copy):
        copy.start()
        started.append(copy)
        return copy

    for p in (0, 1):
        for d in range(1, zs):
            mine = bufs[p].at[c, x, y, z]
            go(remote(mine, mine, gz_send.at[p, d], gz_recv.at[p, d], z_peers[d - 1]))

    def wait_z(p):
        for d in range(1, zs):
            there = bufs[p].at[c, x, y, lax.rem(z + zs - d, zs)]
            remote(there, there, gz_send.at[p, d], gz_recv.at[p, d], z_peers[d - 1]).wait_recv()

    def exchange(p, stage, mine, theirs, peer):
        go(remote(mine, mine, g_send.at[p, stage], g_recv.at[p, stage], peer))
        return remote(theirs, theirs, g_send.at[p, stage], g_recv.at[p, stage], peer)

    wait_z(0)
    first_a = exchange(0, 0, buf_a.at[c, x, y], buf_a.at[c, x, 1 - y], y_peer)
    wait_z(1)
    first_b = exchange(1, 0, buf_b.at[c, x, y], buf_b.at[c, 1 - x, y], x_peer)
    first_a.wait_recv()
    second_a = exchange(0, 1, buf_a.at[c, x], buf_a.at[c, 1 - x], x_peer)
    first_b.wait_recv()
    second_b = exchange(1, 1, buf_b.at[c, :, y], buf_b.at[c, :, 1 - y], y_peer)
    second_a.wait_recv()
    third_a = exchange(0, 2, buf_a.at[c], buf_a.at[1 - c], c_peer)
    second_b.wait_recv()
    third_b = exchange(1, 2, buf_b.at[c], buf_b.at[1 - c], c_peer)
    load_in.wait()

    count = 4 * zs * rows

    def flat(block):
        return block.astype(F32).reshape(count, block.shape[-1])

    def first_product(index, slot):
        xa = flat(buf_a[index]).astype(BF16)
        xb = flat(buf_b[index, :, :, :, :, :half]).astype(BF16)
        h = jnp.dot(xa, win[:half, :], preferred_element_type=F32)
        h = h + jnp.dot(xb, win[half:, :], preferred_element_type=F32)
        act[slot] = (h / (1.0 + jnp.exp(-h))).astype(BF16)
        tab = flat(buf_b[index, :, :, :, :, half:])
        column = lax.broadcasted_iota(jnp.int32, tab.shape, 1)
        g = jnp.sum(jnp.where(column == e, tab, 0.0), axis=1, keepdims=True)
        gate[slot] = jnp.broadcast_to(g, (count, 128))

    first_product(c, 0)
    third_a.wait_recv()
    third_b.wait_recv()
    first_product(1 - c, 1)
    load_out.wait()

    def second_product(p, slot):
        w = wout[:, p * half : (p + 1) * half]
        return jnp.dot(act[slot], w, preferred_element_type=F32) * gate[slot][:, :1]

    def send(p, stage, src, dst, peer):
        return go(remote(src, dst, r_send.at[p, stage], r_recv.at[p, stage], peer))

    core = []
    for p in (0, 1):
        value = second_product(p, 1)
        cs[p][...] = value.reshape(cs[p].shape).astype(BF16)
        core.append(send(p, 0, cs[p], cr[p], c_peer))
    one = []
    for p in (0, 1):
        acc[p][...] = second_product(p, 0).reshape(acc[p].shape)
    for p in (0, 1):
        core[p].wait_recv()
        if p == 0:
            away = acc[p][1 - x] + cr[p][1 - x].astype(F32)
        else:
            away = acc[p][:, 1 - y] + cr[p][:, 1 - y].astype(F32)
        s1[p][...] = away.astype(BF16)
        one.append(send(p, 1, s1[p], r1[p], x_peer if p == 0 else y_peer))
        if p == 0:
            k1[p][...] = acc[p][x] + cr[p][x].astype(F32)
        else:
            k1[p][...] = acc[p][:, y] + cr[p][:, y].astype(F32)
    two = []
    for p in (0, 1):
        one[p].wait_recv()
        keep, give, peer = (y, 1 - y, y_peer) if p == 0 else (x, 1 - x, x_peer)
        s2[p][...] = (k1[p][give] + r1[p][give].astype(F32)).astype(BF16)
        two.append(send(p, 2, s2[p], r2[p], peer))
        k2[p][...] = k1[p][keep] + r1[p][keep].astype(F32)
    last = []
    for p in (0, 1):
        two[p].wait_recv()
        total = k2[p][...] + r2[p][...].astype(F32)
        k2[p][...] = total
        s3[p][...] = total.astype(BF16)
        for d in range(1, zs):
            last.append(go(remote(
                s3[p].at[lax.rem(z + d, zs)], r3[p].at[d - 1],
                rz_send.at[p, d], rz_recv.at[p, d], z_peers[d - 1],
            )))
    for p in (0, 1):
        total = k2[p][z]
        for d in range(1, zs):
            last[p * (zs - 1) + d - 1].wait_recv()
            total = total + r3[p][d - 1].astype(F32)
        out_ref[:, p * half : (p + 1) * half] = total.astype(BF16)
    for copy in started:
        copy.wait_send()


def dense_plan(tokens, routes, gate_weights, w_in, w_out):
    zs = lax.axis_size("expert") // 4
    rows, width = tokens.shape
    units = w_in.shape[2]
    half = width // 2
    count = 4 * zs * rows

    def both(lead, dtype, extra=0):
        return [pltpu.VMEM(lead + (rows, half), dtype), pltpu.VMEM(lead + (rows, half + extra), dtype)]

    dma = pltpu.SemaphoreType.DMA
    scratch = (
        both((2, 2, 2, zs), BF16, 128)
        + [pltpu.VMEM((width, units), BF16), pltpu.VMEM((units, width), BF16)]
        + [pltpu.VMEM((2, count, 128), F32), pltpu.VMEM((2, count, units), BF16)]
        + both((2, 2, zs), BF16) + both((2, 2, zs), BF16) + both((2, 2, zs), F32)
        + both((2, zs), BF16) + both((2, zs), BF16) + both((2, zs), F32)
        + both((zs,), BF16) + both((zs,), BF16) + both((zs,), F32)
        + both((zs,), BF16) + both((zs - 1,), BF16)
        + [dma((2,)), dma((2, zs)), dma((2, zs)), dma((2, 3)), dma((2, 3)),
           dma((2, 3)), dma((2, 3)), dma((2, zs)), dma((2, zs))]
    )
    vmem = pl.BlockSpec(memory_space=pltpu.VMEM)
    hbm = pl.BlockSpec(memory_space=pl.ANY)
    return pl.pallas_call(
        functools.partial(dense_kernel, zs),
        out_shape=jax.ShapeDtypeStruct((rows, width), BF16),
        in_specs=[vmem, vmem, vmem, hbm, hbm],
        out_specs=vmem,
        scratch_shapes=scratch,
        compiler_params=pltpu.CompilerParams(
            collective_id=0, has_side_effects=True, vmem_limit_bytes=48 * 2**20
        ),
        cost_estimate=pl.CostEstimate(
            flops=8 * count * width * units,
            bytes_accessed=4 * width * units,
            transcendentals=2 * count * units,
        ),
    )(tokens, routes, gate_weights, w_in, w_out)


def solution(mesh):
    experts, parts = mesh.shape["expert"], mesh.shape["hidden"]

    def per_device(tokens, routes, gate_weights, w_in, w_out):
        group = tokens.shape[0] * parts
        named = w_in.shape[0] * experts
        capacity = min(group, 2 * group * routes.shape[1] // named)
        dense = (
            capacity == group and parts == 2 and experts % 4 == 0 and w_in.shape[0] == 1
            and 8 <= experts <= 16 and tokens.shape[0] == 8 and tokens.shape[1] % 256 == 0
        )
        plan = dense_plan if dense else routed_plan
        return plan(tokens, routes, gate_weights, w_in, w_out)

    placed = (
        P(("expert", "hidden"), None),
        P(("expert", "hidden"), None),
        P(("expert", "hidden"), None),
        P("expert", None, "hidden"),
        P("expert", "hidden", None),
    )
    return jax.shard_map(
        per_device,
        mesh=mesh,
        in_specs=placed,
        out_specs=P(("expert", "hidden"), None),
        check_vma=False,
    )
```

```python
import functools

import jax
import jax.numpy as jnp
from jax import lax
from jax.experimental import pallas as pl
from jax.experimental.pallas import tpu as pltpu
from jax.sharding import PartitionSpec as P

MESH = pl.DeviceIdType.MESH
F32 = jnp.float32
BF16 = jnp.bfloat16


def routed_plan(tokens, routes, gate_weights, w_in, w_out):
    group_x, group_routes, group_gates = (
        lax.all_gather(tokens, "hidden", axis=0, tiled=True),
        lax.all_gather(routes, "hidden", axis=0, tiled=True),
        lax.all_gather(gate_weights, "hidden", axis=0, tiled=True),
    )
    group = group_x.shape[0]
    top = group_routes.shape[1]
    experts = w_in.shape[0] * lax.axis_size("expert")
    capacity = min(group, 2 * group * top // experts)
    items = group * top
    expert_ids = group_routes.reshape(items)
    onehot = (expert_ids[:, None] == jnp.arange(experts, dtype=jnp.int32)[None, :]).astype(
        jnp.int32
    )
    before = jnp.cumsum(onehot, axis=0) - onehot
    rank = jnp.sum(before * onehot, axis=1)
    slot = expert_ids * capacity + rank
    token_of_item = jnp.arange(items, dtype=jnp.int32) // top
    match = slot[None, :] == jnp.arange(experts * capacity, dtype=jnp.int32)[:, None]
    source_row = jnp.sum(jnp.where(match, token_of_item[None, :], 0), axis=1)
    filled = jnp.any(match, axis=1)
    buffer = jnp.where(filled[:, None], group_x[source_row], jnp.zeros((), jnp.bfloat16))
    buffer = buffer.reshape(experts, capacity, group_x.shape[1])
    first = w_in[0]
    second = w_out[0]
    rows = lax.all_to_all(buffer, "expert", split_axis=0, concat_axis=0, tiled=True)
    count = rows.shape[0] * rows.shape[1]
    flat = rows.reshape(count, rows.shape[2])
    hidden = jax.nn.silu(jnp.dot(flat, first, preferred_element_type=jnp.float32)).astype(
        jnp.bfloat16
    )
    partial_value = jnp.dot(hidden, second, preferred_element_type=jnp.float32)
    partial_value = partial_value.reshape(rows.shape[0], rows.shape[1], partial_value.shape[1])
    gates_flat = group_gates.reshape(items).astype(jnp.float32)
    summed = lax.psum_scatter(
        partial_value.astype(jnp.bfloat16), "hidden", scatter_dimension=2, tiled=True
    ).astype(jnp.float32)
    back = lax.all_to_all(
        summed.astype(jnp.bfloat16), "expert", split_axis=0, concat_axis=0, tiled=True
    ).astype(summed.dtype)
    width = back.shape[2]
    picked = back.reshape(experts * capacity, width)[slot]
    mixed_part = jnp.sum((picked * gates_flat[:, None]).reshape(group, top, width), axis=1)
    result = lax.all_to_all(
        mixed_part.astype(jnp.bfloat16), "hidden", split_axis=0, concat_axis=1, tiled=True
    ).astype(mixed_part.dtype)
    return result.astype(jnp.bfloat16)


SIZES = (6, 6, 5, 5, 3, 3)
ORDERS = (("z", "x", "y"), ("z", "y", "x"), ("z", "x", "y"), ("z", "y", "x"), ("x", "y", "z"), ("y", "x", "z"))
FIRST = (4, 5, 1, 0, 2, 3)
GATHER_STEPS = (
    (4, 0), (5, 0), (4, 1), (5, 1), (1, 0), (0, 0), (2, 0), (3, 0), (0, 1), (1, 1), (2, 1), (3, 1),
    (0, 2), (1, 2), (2, 2), (3, 2), (4, 2), (5, 2),
)
REDUCE_STEPS = (
    (0, 0), (1, 0), (4, 0), (5, 0), (2, 0), (3, 0), (0, 1), (1, 1), (2, 1), (3, 1), (0, 2), (1, 2),
    (4, 1), (5, 1), (4, 2), (5, 2), (2, 2), (3, 2),
)
GATE_PART = 5
DIMS = ("x", "y", "z")


def plan_parts(width):
    tiles, parts, before = width // 128, [], 0
    for size, order in zip(SIZES, ORDERS):
        first = tiles * before // sum(SIZES)
        before += size
        end = tiles * before // sum(SIZES)
        parts.append((first * 128, (end - first) * 128, order))
    return parts


def dense_kernel(
    zs, parts, tok_hbm, routes_hbm, gates_hbm, win_hbm, wout_hbm, out_ref,
    bufs, states, core_bufs, stage_bufs, routes_ref, gates_ref, win, wout, xs, gate, act,
    w_sem, t_sem, g_send, g_recv, r_send, r_recv,
):
    e = lax.axis_index("expert")
    c = lax.rem(e, 2)
    here = {"x": lax.axis_index("hidden"), "y": lax.rem(e // 2, 2), "z": e // 4}
    size = {"x": 2, "y": 2, "z": zs}
    rows, width = tok_hbm.shape
    top = routes_hbm.shape[1]

    def device(at, core):
        return ((at["z"] * 2 + at["y"]) * 2 + core, at["x"])

    def moved(dim, d):
        return lax.rem(here[dim] + d, size[dim])

    def peer(dim, d):
        return device({**here, dim: moved(dim, d)}, c)

    c_peer = device(here, 1 - c)

    small = [
        pltpu.make_async_copy(routes_hbm, routes_ref, w_sem.at[2]),
        pltpu.make_async_copy(gates_hbm, gates_ref, w_sem.at[3]),
    ]
    for p, (first, columns, _) in enumerate(parts):
        small.append(pltpu.make_async_copy(
            tok_hbm.at[:, pl.ds(first, columns)],
            bufs[p].at[c, here["x"], here["y"], here["z"], :, pl.ds(0, columns)],
            t_sem.at[p],
        ))
    for copy in small:
        copy.start()
    load_in = pltpu.make_async_copy(win_hbm.at[0], win, w_sem.at[0])
    load_out = pltpu.make_async_copy(wout_hbm.at[0], wout, w_sem.at[1])
    load_in.start()
    load_out.start()

    barrier = pltpu.get_barrier_semaphore()
    greeted = [peer(dim, d) for dim in DIMS for d in range(1, size[dim])] + [c_peer]
    for other in greeted:
        pl.semaphore_signal(barrier, inc=1, device_id=other, device_id_type=MESH)

    for copy in small[2:]:
        copy.wait()

    pl.semaphore_wait(barrier, len(greeted))

    def remote(src, dst, send, recv, to):
        return pltpu.make_async_remote_copy(
            src_ref=src, dst_ref=dst, send_sem=send, recv_sem=recv,
            device_id=to, device_id_type=MESH,
        )

    started = []

    def go(copy):
        copy.start()
        started.append(copy)
        return copy

    def gathered(p, stage, shift):
        order = parts[p][2]
        index = [c]
        for dim in DIMS:
            if dim in order[:stage]:
                index.append(slice(None))
            elif dim == order[stage]:
                index.append(moved(dim, shift))
            else:
                index.append(here[dim])
        return bufs[p].at[tuple(index)]

    def gather_start(p, stage):
        if stage == 3:
            mine = bufs[p].at[c]
            go(remote(mine, mine, g_send.at[p, 3, 0], g_recv.at[p, 3, 0], c_peer))
            return
        dim = parts[p][2][stage]
        mine = gathered(p, stage, 0)
        for d in range(1, size[dim]):
            go(remote(
                mine, mine, g_send.at[p, stage, d - 1], g_recv.at[p, stage, d - 1], peer(dim, d)
            ))

    def gather_wait(p, stage):
        if stage == 3:
            there = bufs[p].at[1 - c]
            remote(there, there, g_send.at[p, 3, 0], g_recv.at[p, 3, 0], c_peer).wait_recv()
            return
        dim = parts[p][2][stage]
        for d in range(1, size[dim]):
            there = gathered(p, stage, size[dim] - d)
            remote(
                there, there, g_send.at[p, stage, d - 1], g_recv.at[p, stage, d - 1], peer(dim, d)
            ).wait_recv()

    for p in FIRST:
        if p != GATE_PART:
            gather_start(p, 0)

    small[0].wait()
    small[1].wait()
    lanes = lax.broadcasted_iota(jnp.int32, (rows, 128), 1)
    table = jnp.zeros((rows, 128), F32)
    routes = routes_ref[...]
    gates = gates_ref[...].astype(F32)
    for k in range(top):
        table = table + jnp.where(lanes == routes[:, k : k + 1], gates[:, k : k + 1], 0.0)
    own = (c, here["x"], here["y"], here["z"])
    tail = parts[GATE_PART][1]
    bufs[GATE_PART][own + (slice(None), slice(tail, tail + 128))] = table.astype(BF16)
    gather_start(GATE_PART, 0)
    for p, stage in GATHER_STEPS:
        gather_wait(p, stage)
        gather_start(p, stage + 1)
    load_in.wait()

    count = 4 * zs * rows

    def flat(block):
        return block.astype(F32).reshape(count, block.shape[-1])

    def first_product(half, slot):
        for p, (first, columns, _) in enumerate(parts):
            block = bufs[p][half, :, :, :, :, :columns]
            xs[:, first : first + columns] = flat(block).astype(BF16)
        h = jnp.dot(xs[...], win[...], preferred_element_type=F32)
        act[slot] = (h / (1.0 + jnp.exp(-h))).astype(BF16)
        tab = flat(bufs[GATE_PART][half, :, :, :, :, tail : tail + 128])
        column = lax.broadcasted_iota(jnp.int32, tab.shape, 1)
        g = jnp.sum(jnp.where(column == e, tab, 0.0), axis=1, keepdims=True)
        gate[slot] = jnp.broadcast_to(g, (count, 128))

    first_product(c, 0)
    for p in range(len(parts)):
        gather_wait(p, 3)
    first_product(1 - c, 1)
    load_out.wait()

    def second_product(p, slot):
        first, columns, _ = parts[p]
        w = wout[:, first : first + columns]
        return jnp.dot(act[slot], w, preferred_element_type=F32) * gate[slot][:, :1]

    arriving = {}
    for p in range(len(parts)):
        give, take = core_bufs[p]
        give[...] = second_product(p, 1).reshape(give.shape).astype(BF16)
        arriving[p] = [(go(remote(give, take, r_send.at[p, 3, 0], r_recv.at[p, 3, 0], c_peer)), take)]

    def reduce_step(p, stage):
        order = parts[p][2][::-1]
        dim = order[stage]
        left = [d for d in DIMS if d not in order[:stage]]
        if stage == 0:
            states[p][0][...] = second_product(p, 0).reshape(states[p][0].shape)
        for copy, _ in arriving[p]:
            copy.wait_recv()
        coming = [ref for _, ref in arriving[p]]

        def take(shift):
            index = tuple(moved(d, shift) if d == dim else slice(None) for d in left)
            total = states[p][stage][index]
            for ref in coming:
                total = total + ref[index].astype(F32)
            return total

        give, room = stage_bufs[p][stage]
        sent = []
        for d in range(1, size[dim]):
            give[d - 1] = take(d).astype(BF16)
            sent.append((go(remote(
                give.at[d - 1], room.at[d - 1],
                r_send.at[p, stage, d - 1], r_recv.at[p, stage, d - 1], peer(dim, d),
            )), room.at[d - 1]))
        states[p][stage + 1][...] = take(0)
        arriving[p] = sent

    for p, stage in REDUCE_STEPS:
        reduce_step(p, stage)
    for p, (first, columns, _) in enumerate(parts):
        total = states[p][3][...]
        for copy, ref in arriving[p]:
            copy.wait_recv()
            total = total + ref[...].astype(F32)
        out_ref[:, first : first + columns] = total.astype(BF16)
    for copy in started:
        copy.wait_send()


def dense_plan(tokens, routes, gate_weights, w_in, w_out):
    zs = lax.axis_size("expert") // 4
    rows, width = tokens.shape
    units = w_in.shape[2]
    count = 4 * zs * rows
    size = {"x": 2, "y": 2, "z": zs}
    parts = plan_parts(width)
    dma = pltpu.SemaphoreType.DMA

    bufs, states, core_bufs, stage_bufs = [], [], [], []
    for p, (_, columns, order) in enumerate(parts):
        extra = 128 if p == GATE_PART else 0
        bufs.append(pltpu.VMEM((2, 2, 2, zs, rows, columns + extra), BF16))
        left = list(DIMS)

        def shape(lead=()):
            return lead + tuple(size[d] for d in left) + (rows, columns)

        core_bufs.append((pltpu.VMEM(shape(), BF16), pltpu.VMEM(shape(), BF16)))
        state, stages = [pltpu.VMEM(shape(), F32)], []
        for dim in order[::-1]:
            left.remove(dim)
            lead = (size[dim] - 1,)
            stages.append((pltpu.VMEM(shape(lead), BF16), pltpu.VMEM(shape(lead), BF16)))
            state.append(pltpu.VMEM(shape(), F32))
        states.append(tuple(state))
        stage_bufs.append(tuple(stages))
    n = len(parts)
    scratch = (
        tuple(bufs), tuple(states), tuple(core_bufs), tuple(stage_bufs),
        pltpu.VMEM(routes.shape, routes.dtype), pltpu.VMEM(gate_weights.shape, BF16),
        pltpu.VMEM((width, units), BF16), pltpu.VMEM((units, width), BF16),
        pltpu.VMEM((count, width), BF16),
        pltpu.VMEM((2, count, 128), F32), pltpu.VMEM((2, count, units), BF16),
        dma((4,)), dma((n,)),
        dma((n, 4, zs - 1)), dma((n, 4, zs - 1)), dma((n, 4, zs - 1)), dma((n, 4, zs - 1)),
    )
    hbm = pl.BlockSpec(memory_space=pltpu.HBM)
    return pl.pallas_call(
        functools.partial(dense_kernel, zs, parts),
        out_shape=jax.ShapeDtypeStruct((rows, width), BF16),
        in_specs=[hbm] * 5,
        out_specs=pl.BlockSpec(memory_space=pltpu.VMEM),
        scratch_shapes=scratch,
        compiler_params=pltpu.CompilerParams(
            collective_id=0, has_side_effects=True, vmem_limit_bytes=64 * 2**20
        ),
        cost_estimate=pl.CostEstimate(
            flops=8 * count * width * units,
            bytes_accessed=4 * width * units,
            transcendentals=2 * count * units,
        ),
    )(tokens, routes, gate_weights, w_in, w_out)


def solution(mesh):
    experts, parts = mesh.shape["expert"], mesh.shape["hidden"]

    def per_device(tokens, routes, gate_weights, w_in, w_out):
        group = tokens.shape[0] * parts
        named = w_in.shape[0] * experts
        capacity = min(group, 2 * group * routes.shape[1] // named)
        dense = (
            capacity == group and parts == 2 and experts % 4 == 0 and w_in.shape[0] == 1
            and 8 <= experts <= 16 and tokens.shape[0] == 8 and tokens.shape[1] % 128 == 0 and tokens.shape[1] >= 1024
        )
        plan = dense_plan if dense else routed_plan
        return plan(tokens, routes, gate_weights, w_in, w_out)

    placed = (
        P(("expert", "hidden"), None),
        P(("expert", "hidden"), None),
        P(("expert", "hidden"), None),
        P("expert", None, "hidden"),
        P("expert", "hidden", None),
    )
    return jax.shard_map(
        per_device,
        mesh=mesh,
        in_specs=placed,
        out_specs=P(("expert", "hidden"), None),
        check_vma=False,
    )
```

```python
import functools

import jax
import jax.numpy as jnp
from jax import lax
from jax.experimental import pallas as pl
from jax.experimental.pallas import tpu as pltpu
from jax.sharding import PartitionSpec as P

MESH = pl.DeviceIdType.MESH
F32 = jnp.float32
BF16 = jnp.bfloat16


def routed_plan(tokens, routes, gate_weights, w_in, w_out):
    group_x, group_routes, group_gates = (
        lax.all_gather(tokens, "hidden", axis=0, tiled=True),
        lax.all_gather(routes, "hidden", axis=0, tiled=True),
        lax.all_gather(gate_weights, "hidden", axis=0, tiled=True),
    )
    group = group_x.shape[0]
    top = group_routes.shape[1]
    experts = w_in.shape[0] * lax.axis_size("expert")
    capacity = min(group, 2 * group * top // experts)
    items = group * top
    expert_ids = group_routes.reshape(items)
    onehot = (expert_ids[:, None] == jnp.arange(experts, dtype=jnp.int32)[None, :]).astype(
        jnp.int32
    )
    before = jnp.cumsum(onehot, axis=0) - onehot
    rank = jnp.sum(before * onehot, axis=1)
    slot = expert_ids * capacity + rank
    token_of_item = jnp.arange(items, dtype=jnp.int32) // top
    match = slot[None, :] == jnp.arange(experts * capacity, dtype=jnp.int32)[:, None]
    source_row = jnp.sum(jnp.where(match, token_of_item[None, :], 0), axis=1)
    filled = jnp.any(match, axis=1)
    buffer = jnp.where(filled[:, None], group_x[source_row], jnp.zeros((), jnp.bfloat16))
    buffer = buffer.reshape(experts, capacity, group_x.shape[1])
    first = w_in[0]
    second = w_out[0]
    rows = lax.all_to_all(buffer, "expert", split_axis=0, concat_axis=0, tiled=True)
    count = rows.shape[0] * rows.shape[1]
    flat = rows.reshape(count, rows.shape[2])
    hidden = jax.nn.silu(jnp.dot(flat, first, preferred_element_type=jnp.float32)).astype(
        jnp.bfloat16
    )
    partial_value = jnp.dot(hidden, second, preferred_element_type=jnp.float32)
    partial_value = partial_value.reshape(rows.shape[0], rows.shape[1], partial_value.shape[1])
    gates_flat = group_gates.reshape(items).astype(jnp.float32)
    summed = lax.psum_scatter(
        partial_value.astype(jnp.bfloat16), "hidden", scatter_dimension=2, tiled=True
    ).astype(jnp.float32)
    back = lax.all_to_all(
        summed.astype(jnp.bfloat16), "expert", split_axis=0, concat_axis=0, tiled=True
    ).astype(summed.dtype)
    width = back.shape[2]
    picked = back.reshape(experts * capacity, width)[slot]
    mixed_part = jnp.sum((picked * gates_flat[:, None]).reshape(group, top, width), axis=1)
    result = lax.all_to_all(
        mixed_part.astype(jnp.bfloat16), "hidden", split_axis=0, concat_axis=1, tiled=True
    ).astype(mixed_part.dtype)
    return result.astype(jnp.bfloat16)


SIZES = (6, 6, 5, 5, 3, 3)
ORDERS = (("z", "x", "y"), ("z", "y", "x"), ("z", "x", "y"), ("z", "y", "x"), ("x", "y", "z"), ("y", "x", "z"))
FIRST = (0, 1, 4, 2, 3, 5)
GATHER_STEPS = (
    (4, 0), (5, 0), (0, 0), (1, 0), (2, 0), (3, 0), (4, 1), (5, 1), (0, 1), (1, 1), (2, 1), (3, 1),
    (0, 2), (1, 2), (2, 2), (3, 2), (4, 2), (5, 2),
)
REDUCE_STEPS = (
    (0, 0), (1, 0), (4, 0), (5, 0), (2, 0), (3, 0), (0, 1), (1, 1), (2, 1), (3, 1), (0, 2), (1, 2),
    (4, 1), (5, 1), (4, 2), (5, 2), (2, 2), (3, 2),
)
GATE_PART = 5
DIMS = ("x", "y", "z")


def plan_parts(width):
    tiles, parts, before = width // 128, [], 0
    for size, order in zip(SIZES, ORDERS):
        first = tiles * before // sum(SIZES)
        before += size
        end = tiles * before // sum(SIZES)
        parts.append((first * 128, (end - first) * 128, order))
    return parts


def dense_kernel(
    zs, parts, tok_hbm, routes_hbm, gates_hbm, win_hbm, wout_hbm, out_ref,
    bufs, states, core_bufs, stage_bufs, routes_ref, gates_ref, win, wout, xs, gate, act,
    w_sem, t_sem, g_send, g_recv, r_send, r_recv,
):
    e = lax.axis_index("expert")
    c = lax.rem(e, 2)
    here = {"x": lax.axis_index("hidden"), "y": lax.rem(e // 2, 2), "z": e // 4}
    size = {"x": 2, "y": 2, "z": zs}
    rows, width = tok_hbm.shape
    top = routes_hbm.shape[1]

    def device(at, core):
        return ((at["z"] * 2 + at["y"]) * 2 + core, at["x"])

    def moved(dim, d):
        return lax.rem(here[dim] + d, size[dim])

    def peer(dim, d):
        return device({**here, dim: moved(dim, d)}, c)

    c_peer = device(here, 1 - c)

    small = [
        pltpu.make_async_copy(routes_hbm, routes_ref, w_sem.at[2]),
        pltpu.make_async_copy(gates_hbm, gates_ref, w_sem.at[3]),
    ]
    for p, (first, columns, _) in enumerate(parts):
        small.append(pltpu.make_async_copy(
            tok_hbm.at[:, pl.ds(first, columns)],
            bufs[p].at[c, here["x"], here["y"], here["z"], :, pl.ds(0, columns)],
            t_sem.at[p],
        ))
    for copy in small:
        copy.start()
    load_in = pltpu.make_async_copy(win_hbm.at[0], win, w_sem.at[0])
    load_out = pltpu.make_async_copy(wout_hbm.at[0], wout, w_sem.at[1])
    load_in.start()
    load_out.start()

    barrier = pltpu.get_barrier_semaphore()
    greeted = [peer(dim, d) for dim in DIMS for d in range(1, size[dim])] + [c_peer]
    for other in greeted:
        pl.semaphore_signal(barrier, inc=1, device_id=other, device_id_type=MESH)

    for copy in small[2:]:
        copy.wait()

    pl.semaphore_wait(barrier, len(greeted))

    def remote(src, dst, send, recv, to):
        return pltpu.make_async_remote_copy(
            src_ref=src, dst_ref=dst, send_sem=send, recv_sem=recv,
            device_id=to, device_id_type=MESH,
        )

    started = []

    def go(copy):
        copy.start()
        started.append(copy)
        return copy

    def gathered(p, stage, shift):
        order = parts[p][2]
        index = [c]
        for dim in DIMS:
            if dim in order[:stage]:
                index.append(slice(None))
            elif dim == order[stage]:
                index.append(moved(dim, shift))
            else:
                index.append(here[dim])
        return bufs[p].at[tuple(index)]

    def gather_start(p, stage):
        if stage == 3:
            mine = bufs[p].at[c]
            go(remote(mine, mine, g_send.at[p, 3, 0], g_recv.at[p, 3, 0], c_peer))
            return
        dim = parts[p][2][stage]
        mine = gathered(p, stage, 0)
        for d in range(1, size[dim]):
            go(remote(
                mine, mine, g_send.at[p, stage, d - 1], g_recv.at[p, stage, d - 1], peer(dim, d)
            ))

    def gather_wait(p, stage):
        if stage == 3:
            there = bufs[p].at[1 - c]
            remote(there, there, g_send.at[p, 3, 0], g_recv.at[p, 3, 0], c_peer).wait_recv()
            return
        dim = parts[p][2][stage]
        for d in range(1, size[dim]):
            there = gathered(p, stage, size[dim] - d)
            remote(
                there, there, g_send.at[p, stage, d - 1], g_recv.at[p, stage, d - 1], peer(dim, d)
            ).wait_recv()

    for p in FIRST:
        if p != GATE_PART:
            gather_start(p, 0)

    small[0].wait()
    small[1].wait()
    lanes = lax.broadcasted_iota(jnp.int32, (rows, 128), 1)
    table = jnp.zeros((rows, 128), F32)
    routes = routes_ref[...]
    gates = gates_ref[...].astype(F32)
    for k in range(top):
        table = table + jnp.where(lanes == routes[:, k : k + 1], gates[:, k : k + 1], 0.0)
    own = (c, here["x"], here["y"], here["z"])
    tail = parts[GATE_PART][1]
    bufs[GATE_PART][own + (slice(None), slice(tail, tail + 128))] = table.astype(BF16)
    gather_start(GATE_PART, 0)
    for p, stage in GATHER_STEPS:
        gather_wait(p, stage)
        gather_start(p, stage + 1)
    load_in.wait()

    count = 4 * zs * rows

    def flat(block):
        return block.astype(F32).reshape(count, block.shape[-1])

    def first_product(half, slot):
        for p, (first, columns, _) in enumerate(parts):
            block = bufs[p][half, :, :, :, :, :columns]
            xs[:, first : first + columns] = flat(block).astype(BF16)
        h = jnp.dot(xs[...], win[...], preferred_element_type=F32)
        act[slot] = (h / (1.0 + jnp.exp(-h))).astype(BF16)
        tab = flat(bufs[GATE_PART][half, :, :, :, :, tail : tail + 128])
        column = lax.broadcasted_iota(jnp.int32, tab.shape, 1)
        g = jnp.sum(jnp.where(column == e, tab, 0.0), axis=1, keepdims=True)
        gate[slot] = jnp.broadcast_to(g, (count, 128))

    first_product(c, 0)
    for p in range(len(parts)):
        gather_wait(p, 3)
    first_product(1 - c, 1)
    load_out.wait()

    def second_product(p, slot):
        first, columns, _ = parts[p]
        w = wout[:, first : first + columns]
        return jnp.dot(act[slot], w, preferred_element_type=F32) * gate[slot][:, :1]

    arriving = {}
    for p in range(len(parts)):
        give, take = core_bufs[p]
        give[...] = second_product(p, 1).reshape(give.shape).astype(BF16)
        arriving[p] = [(go(remote(give, take, r_send.at[p, 3, 0], r_recv.at[p, 3, 0], c_peer)), take)]

    def reduce_step(p, stage):
        order = parts[p][2][::-1]
        dim = order[stage]
        left = [d for d in DIMS if d not in order[:stage]]
        if stage == 0:
            states[p][0][...] = second_product(p, 0).reshape(states[p][0].shape)
        for copy, _ in arriving[p]:
            copy.wait_recv()
        coming = [ref for _, ref in arriving[p]]

        def take(shift):
            index = tuple(moved(d, shift) if d == dim else slice(None) for d in left)
            total = states[p][stage][index]
            for ref in coming:
                total = total + ref[index].astype(F32)
            return total

        give, room = stage_bufs[p][stage]
        sent = []
        for d in range(1, size[dim]):
            give[d - 1] = take(d).astype(BF16)
            sent.append((go(remote(
                give.at[d - 1], room.at[d - 1],
                r_send.at[p, stage, d - 1], r_recv.at[p, stage, d - 1], peer(dim, d),
            )), room.at[d - 1]))
        states[p][stage + 1][...] = take(0)
        arriving[p] = sent

    for p, stage in REDUCE_STEPS:
        reduce_step(p, stage)
    for p, (first, columns, _) in enumerate(parts):
        total = states[p][3][...]
        for copy, ref in arriving[p]:
            copy.wait_recv()
            total = total + ref[...].astype(F32)
        out_ref[:, first : first + columns] = total.astype(BF16)
    for copy in started:
        copy.wait_send()


def dense_plan(tokens, routes, gate_weights, w_in, w_out):
    zs = lax.axis_size("expert") // 4
    rows, width = tokens.shape
    units = w_in.shape[2]
    count = 4 * zs * rows
    size = {"x": 2, "y": 2, "z": zs}
    parts = plan_parts(width)
    dma = pltpu.SemaphoreType.DMA

    bufs, states, core_bufs, stage_bufs = [], [], [], []
    for p, (_, columns, order) in enumerate(parts):
        extra = 128 if p == GATE_PART else 0
        bufs.append(pltpu.VMEM((2, 2, 2, zs, rows, columns + extra), BF16))
        left = list(DIMS)

        def shape(lead=()):
            return lead + tuple(size[d] for d in left) + (rows, columns)

        core_bufs.append((pltpu.VMEM(shape(), BF16), pltpu.VMEM(shape(), BF16)))
        state, stages = [pltpu.VMEM(shape(), F32)], []
        for dim in order[::-1]:
            left.remove(dim)
            lead = (size[dim] - 1,)
            stages.append((pltpu.VMEM(shape(lead), BF16), pltpu.VMEM(shape(lead), BF16)))
            state.append(pltpu.VMEM(shape(), F32))
        states.append(tuple(state))
        stage_bufs.append(tuple(stages))
    n = len(parts)
    scratch = (
        tuple(bufs), tuple(states), tuple(core_bufs), tuple(stage_bufs),
        pltpu.VMEM(routes.shape, routes.dtype), pltpu.VMEM(gate_weights.shape, BF16),
        pltpu.VMEM((width, units), BF16), pltpu.VMEM((units, width), BF16),
        pltpu.VMEM((count, width), BF16),
        pltpu.VMEM((2, count, 128), F32), pltpu.VMEM((2, count, units), BF16),
        dma((4,)), dma((n,)),
        dma((n, 4, zs - 1)), dma((n, 4, zs - 1)), dma((n, 4, zs - 1)), dma((n, 4, zs - 1)),
    )
    hbm = pl.BlockSpec(memory_space=pltpu.HBM)
    return pl.pallas_call(
        functools.partial(dense_kernel, zs, parts),
        out_shape=jax.ShapeDtypeStruct((rows, width), BF16),
        in_specs=[hbm] * 5,
        out_specs=pl.BlockSpec(memory_space=pltpu.VMEM),
        scratch_shapes=scratch,
        compiler_params=pltpu.CompilerParams(
            collective_id=0, has_side_effects=True, vmem_limit_bytes=64 * 2**20
        ),
        cost_estimate=pl.CostEstimate(
            flops=8 * count * width * units,
            bytes_accessed=4 * width * units,
            transcendentals=2 * count * units,
        ),
    )(tokens, routes, gate_weights, w_in, w_out)


def solution(mesh):
    experts, parts = mesh.shape["expert"], mesh.shape["hidden"]

    def per_device(tokens, routes, gate_weights, w_in, w_out):
        group = tokens.shape[0] * parts
        named = w_in.shape[0] * experts
        capacity = min(group, 2 * group * routes.shape[1] // named)
        dense = (
            capacity == group and parts == 2 and experts % 4 == 0 and w_in.shape[0] == 1
            and 8 <= experts <= 16 and tokens.shape[0] == 8 and tokens.shape[1] % 128 == 0 and tokens.shape[1] >= 1024
        )
        plan = dense_plan if dense else routed_plan
        return plan(tokens, routes, gate_weights, w_in, w_out)

    placed = (
        P(("expert", "hidden"), None),
        P(("expert", "hidden"), None),
        P(("expert", "hidden"), None),
        P("expert", None, "hidden"),
        P("expert", "hidden", None),
    )
    return jax.shard_map(
        per_device,
        mesh=mesh,
        in_specs=placed,
        out_specs=P(("expert", "hidden"), None),
        check_vma=False,
    )
```
